128 devices in a mesh: circ: 16 (over x_lo, y, core), axial: 8 (over z, x_hi).
Axes of the slice: x: 4 (x_hi: 2, x_lo: 2; x = x_hi * 2 + x_lo), y: 4, z: 4, core: 2. Of those that a mesh axis runs over, the one named last changes fastest.
Arguments:
- dual_blocks: bfloat16 [16, 8, 8, 768, 768], P('circ', 'axial'), as said below
- gap_blocks: bfloat16 [16, 8, 8, 768, 768], P('circ', 'axial'), as said below
- gap_list: int32 [16, 8, 8], P('circ', 'axial'), may hold values from 0 to 7, as said below
- gap_target: int32 [16, 8, 8], P('circ', 'axial'), may hold values from 0 to 7, as said below
- gap_count: int32 [16, 8], P('circ', 'axial'), may hold values from 0 to 8, as said below
- face_map: int32 [16, 8, 4, 1024], P('circ', 'axial'), may hold values from 0 to 6143, as said below
- dual_right: float32 [16, 8, 64, 6144], P('circ', 'axial'), may hold values from -6 to 6
Outputs:
- dual_iterate: float32 [16, 8, 64, 6144], P('circ', 'axial')
The draws below stay inside these ranges and needn't reach their ends.
Inputs may be any that keep to these rules, and one draw needn't show every extreme that they name: Slots 0 to gap_count - 1 of a cluster are live; some cluster has all 8 live. `gap_list`: the 8 entries of one cluster name distinct subdomains. `gap_target`: the 8 entries of one cluster name distinct subdomains, each other than the slot's gap_list entry. `face_map`: the 4096 entries of one cluster are distinct multiplier indices. `dual_blocks`: each block is symmetric. `gap_blocks`: each block is symmetric.
All inputs are finite; a program needn't handle non-finite values.
Results may differ from the reference program's by a relative error of at most 0.0013.
Values may be sent and summed in bfloat16 or wider, within the bound.
No kernel may reach another device: no remote copies, remote signals or barrier semaphores. Data moves between devices by JAX's collectives and lax.ppermute only.
A program may use at most 128 MiB of HBM per device.

```python
import math
import jax
import jax.numpy as jnp
from jax import lax

ORDER = 768
COLUMNS = 64
SUB = 8
GAP = 8
FACE = 1024
ITERS = 6
N_CIRC = 16
N_AXIAL = 8


def symmetric_from(raw, diagonal_values):
    order_size = raw.shape[-1]
    mixed = (raw + jnp.swapaxes(raw, -1, -2)) * (0.7071 * 0.25 / math.sqrt(order_size))
    rows_iota = lax.broadcasted_iota(jnp.int32, raw.shape, raw.ndim - 2)
    cols_iota = lax.broadcasted_iota(jnp.int32, raw.shape, raw.ndim - 1)
    return jnp.where(rows_iota == cols_iota, diagonal_values[..., None], mixed)


def draw_dual_blocks(key, part):
    key = jax.random.fold_in(key, 11)
    first_key, second_key = jax.random.split(key)
    shape = (N_CIRC, N_AXIAL, SUB, ORDER, ORDER)
    raw = jax.random.normal(first_key, shape, jnp.float32)
    diagonal_values = jax.random.uniform(second_key, shape[:-1], jnp.float32, 0.8, 1.4)
    return symmetric_from(raw, diagonal_values).astype(jnp.bfloat16)


def draw_gap_blocks(key, part):
    key = jax.random.fold_in(key, 13)
    first_key, second_key = jax.random.split(key)
    shape = (N_CIRC, N_AXIAL, GAP, ORDER, ORDER)
    raw = jax.random.normal(first_key, shape, jnp.float32)
    diagonal_values = jax.random.uniform(second_key, shape[:-1], jnp.float32, 0.8, 1.4)
    return symmetric_from(raw, diagonal_values).astype(jnp.bfloat16)


def draw_gap_count(key, part):
    key = jax.random.fold_in(key, 21)
    first_key, second_key = jax.random.split(key)
    centre = jax.random.randint(first_key, (), 0, N_CIRC)
    circ_position = jnp.arange(N_CIRC, dtype=jnp.int32)
    offset = jnp.abs(circ_position - centre)
    distance = jnp.minimum(offset, N_CIRC - offset)
    jitter = jax.random.randint(second_key, (N_CIRC, N_AXIAL), 0, 3)
    falling = jnp.maximum(GAP - distance[:, None] - jitter, 0)
    return jnp.where(distance[:, None] == 0, GAP, falling).astype(jnp.int32)


def first_of_permutation(one_key, length, taken):
    return jax.random.permutation(one_key, length)[:taken]


def shared_lists(key):
    list_key = jax.random.fold_in(key, 31)
    many_keys = jax.random.split(list_key, N_CIRC * N_AXIAL)
    picked = jax.vmap(lambda single_key: first_of_permutation(single_key, SUB, GAP))(many_keys)
    return picked.reshape(N_CIRC, N_AXIAL, GAP).astype(jnp.int32)


def draw_gap_list(key, part):
    picked = shared_lists(key)
    return picked


def draw_gap_target(key, part):
    picked = shared_lists(key)
    key = jax.random.fold_in(key, 51)
    shift = jax.random.randint(key, (N_CIRC, N_AXIAL, 1), 1, SUB)
    return ((picked + shift) % SUB).astype(jnp.int32)


def draw_face_map(key, part):
    key = jax.random.fold_in(key, 41)
    many_keys = jax.random.split(key, N_CIRC * N_AXIAL)
    picked = jax.vmap(lambda single_key: first_of_permutation(single_key, SUB * ORDER, 4 * FACE))(many_keys)
    return picked.reshape(N_CIRC, N_AXIAL, 4, FACE).astype(jnp.int32)


def steps_of(key, extent, pieces, low, largest):
    loudness, own = 1.0, jax.random.fold_in(key, 6)
    for axis_at, parts in pieces:
        steps = jnp.exp(jax.random.uniform(jax.random.fold_in(own, axis_at), (parts,), jnp.float32, low / len(pieces), largest / len(pieces)))
        loudness = loudness * jnp.repeat(steps, extent[axis_at] // parts).reshape([-1 if axis == axis_at else 1 for axis in range(len(extent))])
    return loudness


def gaussian(stream_key, shape, width, limit, cuts=(), kind=jnp.bfloat16):
    loudness = steps_of(stream_key, shape, cuts, -0.22, 0.18) if cuts else 1.0
    values = jax.random.normal(stream_key, shape, jnp.float32) * width * loudness
    return jnp.minimum(jnp.maximum(values, -limit), limit).astype(kind)


def setup_inputs(seed: int = 0) -> dict:
    key_list = jax.random.split(jax.random.key(seed), 8)
    return {
        "dual_blocks": draw_dual_blocks(jax.random.fold_in(key_list[7], 71), 0),
        "gap_blocks": draw_gap_blocks(jax.random.fold_in(key_list[7], 71), 0),
        "gap_list": draw_gap_list(jax.random.fold_in(key_list[7], 71), 0),
        "gap_target": draw_gap_target(jax.random.fold_in(key_list[7], 71), 0),
        "gap_count": draw_gap_count(jax.random.fold_in(key_list[7], 71), 0),
        "face_map": draw_face_map(jax.random.fold_in(key_list[7], 71), 0),
        "dual_right": gaussian(key_list[6], (N_CIRC, N_AXIAL, COLUMNS, SUB * ORDER), 1.0, 6.0, ((0, 16), (1, 8)), jnp.float32),
    }


relaxation = 0.25


def cluster_products(rounded, blocks, regenerated, chosen, destination, live_count):
    shaped = rounded.astype(jnp.float32).reshape(COLUMNS, SUB, ORDER)
    product = jnp.einsum("ksm,smn->ksn", shaped, blocks.astype(jnp.float32), precision=lax.Precision.HIGHEST)
    for slot_index in range(GAP):
        source = chosen[slot_index].astype(jnp.int32)
        target = destination[slot_index].astype(jnp.int32)
        taken_rows = lax.dynamic_index_in_dim(shaped, source, 1, keepdims=False)
        gap_term = jnp.dot(taken_rows, regenerated[slot_index].astype(jnp.float32), precision=lax.Precision.HIGHEST)
        gap_term = jnp.where(slot_index < live_count, gap_term, jnp.zeros_like(gap_term))
        current = lax.dynamic_index_in_dim(product, target, 1, keepdims=False)
        product = lax.dynamic_update_index_in_dim(product, current + gap_term, target, 1)
    return product.reshape(COLUMNS, SUB * ORDER)


def face_values(applied, face_map, face_number):
    position = face_map[:, :, face_number, :]
    spread = jnp.broadcast_to(position[:, :, None, :], (N_CIRC, N_AXIAL, COLUMNS, FACE))
    return jnp.take_along_axis(applied, spread, axis=3)


def single_add(target_field, position, amount):
    return target_field.at[:, position].add(amount)


def add_faces(applied, face_map, face_number, amount):
    return jax.vmap(jax.vmap(single_add))(applied, face_map[:, :, face_number, :], amount)


def assemble(applied, face_map):
    lower_face = face_values(applied, face_map, 0)
    upper_face = face_values(applied, face_map, 1)
    front_face = face_values(applied, face_map, 2)
    back_face = face_values(applied, face_map, 3)
    from_lower = jnp.roll(upper_face, 1, axis=0)
    from_upper = jnp.roll(lower_face, -1, axis=0)
    zero_rim = jnp.zeros_like(front_face[:, :1])
    from_front = jnp.concatenate([zero_rim, back_face[:, :-1]], axis=1)
    from_back = jnp.concatenate([front_face[:, 1:], zero_rim], axis=1)
    applied = add_faces(applied, face_map, 0, from_lower)
    applied = add_faces(applied, face_map, 1, from_upper)
    applied = add_faces(applied, face_map, 2, from_front)
    applied = add_faces(applied, face_map, 3, from_back)
    return applied


def reference(dual_blocks, gap_blocks, gap_list, gap_target, gap_count, face_map, dual_right):
    clusters = N_CIRC * N_AXIAL
    flat_blocks = dual_blocks.reshape(clusters, SUB, ORDER, ORDER)
    flat_regenerated = gap_blocks.reshape(clusters, GAP, ORDER, ORDER)
    flat_list = gap_list.reshape(clusters, GAP)
    flat_target = gap_target.reshape(clusters, GAP)
    flat_count = gap_count.reshape(clusters)
    iterate = dual_right
    for iteration in range(ITERS):
        rounded = iterate.astype(jnp.bfloat16).reshape(clusters, COLUMNS, SUB * ORDER)
        applied = lax.map(lambda members: cluster_products(*members), (rounded, flat_blocks, flat_regenerated, flat_list, flat_target, flat_count))
        applied = applied.reshape(N_CIRC, N_AXIAL, COLUMNS, SUB * ORDER)
        applied = assemble(applied, face_map)
        iterate = iterate + relaxation * (dual_right - applied)
    return iterate
```

```python
import functools

import jax
import jax.numpy as jnp
from jax import lax
from jax.experimental import pallas as pl
from jax.experimental.pallas import tpu as pltpu
from jax.sharding import PartitionSpec as P

ITERS = 6
RELAXATION = 0.25
UNROLL = 256
LANES = 128


def swap_pairs(count, first, closed):
    pairs = []
    for i in range(first, count, 2):
        if closed or i + 1 < count:
            j = (i + 1) % count
            pairs += [(i, j), (j, i)]
    return pairs


def scatter_faces(index_ref, received, wide, spread):
    spread[...] = jnp.zeros_like(spread)
    half = wide.shape[0] // 2
    columns = LANES // 2
    for f in range(4):
        packed = received[f][...].astype(jnp.float32)
        wide[0:half] = packed
        wide[half:] = pltpu.roll(packed, columns, 1)

        def step(i, carry):
            start = pl.multiple_of(i * UNROLL, UNROLL)
            for u in range(UNROLL):
                spread[pl.ds(index_ref[f, start + u], 1), :] = wide[pl.ds(start + u, 1), :]
            return carry

        lax.fori_loop(0, wide.shape[0] // UNROLL, step, 0)


def gather_faces(index_ref, sends, wide, local):
    half = wide.shape[0] // 2
    columns = LANES // 2
    for f in range(4):

        def step(i, carry):
            start = pl.multiple_of(i * UNROLL, UNROLL)
            for u in range(UNROLL):
                wide[pl.ds(start + u, 1), :] = local[pl.ds(index_ref[f, start + u], 1), :]
            return carry

        lax.fori_loop(0, wide.shape[0] // UNROLL, step, 0)
        low = wide[0:half]
        high = pltpu.roll(wide[half:], columns, 1)
        lane = lax.broadcasted_iota(jnp.int32, low.shape, 1)
        sends[f][...] = jnp.where(lane < columns, low, high).astype(jnp.bfloat16)


def corrected(base_ref, spread, s, order, columns):
    block = spread[s * order:(s + 1) * order, :].T[:columns]
    return base_ref[:, s * order:(s + 1) * order] - RELAXATION * block


def sweep_kernel(first, subs, order, columns, list_ref, target_ref, count_ref, index_ref, dual_ref, gap_ref, right_ref, *rest):
    if first:
        sends, base_out = rest[:4], rest[4]
        iterate, rounded, local, wide, slot_of, source_of = rest[5:]
    else:
        base_ref, received = rest[0], rest[1:5]
        sends, base_out = rest[5:9], rest[9]
        iterate, rounded, local, wide, slot_of, source_of = rest[10:]
    live = count_ref[0, 0]
    for g in range(subs):
        slot_of[target_ref[0, g]] = g
        source_of[target_ref[0, g]] = jnp.where(g < live, list_ref[0, g], subs)
    if not first:
        scatter_faces(index_ref, received, wide, local)
    for s in range(subs):
        if first:
            value = right_ref[:, s * order:(s + 1) * order]
        else:
            value = corrected(base_ref, local, s, order, columns)
            iterate[:, s * order:(s + 1) * order] = value
        rounded[s] = value.astype(jnp.bfloat16)
    rounded[subs] = jnp.zeros_like(rounded[subs])
    for s in range(subs):
        product = jnp.dot(rounded[s], dual_ref[s], preferred_element_type=jnp.float32)
        product += jnp.dot(rounded[source_of[s]], gap_ref[slot_of[s]], preferred_element_type=jnp.float32)
        here = slice(s * order, (s + 1) * order)
        value = right_ref[:, here] if first else iterate[:, here]
        base_out[:, here] = value + RELAXATION * (right_ref[:, here] - product)
        local[here, 0:columns] = product.T
    gather_faces(index_ref, sends, wide, local)


def last_kernel(subs, order, columns, index_ref, base_ref, *rest):
    received, out_ref = rest[:4], rest[4]
    spread, wide = rest[5:]
    scatter_faces(index_ref, received, wide, spread)
    for s in range(subs):
        out_ref[:, s * order:(s + 1) * order] = corrected(base_ref, spread, s, order, columns)


def per_device(dual_blocks, gap_blocks, gap_list, gap_target, gap_count, face_map, dual_right):
    columns, length = dual_right.shape[2:]
    subs, order = dual_blocks.shape[2:4]
    face = face_map.shape[3]
    dual, gap, right = dual_blocks[0, 0], gap_blocks[0, 0], dual_right[0, 0]
    chosen, destination = gap_list[0], gap_target[0]
    n_circ, n_axial = lax.axis_size("circ"), lax.axis_size("axial")
    circ_odd = lax.axis_index("circ") % 2
    axial_odd = lax.axis_index("axial") % 2
    faces = face_map[0, 0]
    circ_faces = jnp.where(circ_odd == 1, faces[0:2], faces[1::-1])
    axial_faces = jnp.where(axial_odd == 1, faces[2:4], faces[3:1:-1])
    index = jnp.concatenate([circ_faces, axial_faces])
    routes = [
        ("circ", swap_pairs(n_circ, 0, True)),
        ("circ", swap_pairs(n_circ, 1, True)),
        ("axial", swap_pairs(n_axial, 0, False)),
        ("axial", swap_pairs(n_axial, 1, False)),
    ]

    vmem = pl.BlockSpec(memory_space=pltpu.VMEM)
    smem = pl.BlockSpec(memory_space=pltpu.SMEM)
    parcel = jax.ShapeDtypeStruct((face // 2, LANES), jnp.bfloat16)
    state = jax.ShapeDtypeStruct((columns, length), jnp.float32)
    rows = pltpu.VMEM((length, LANES), jnp.float32)
    wide = pltpu.VMEM((face, LANES), jnp.float32)
    params = pltpu.CompilerParams(vmem_limit_bytes=16 * 1024 * 1024)

    def sweep(first, *more):
        return pl.pallas_call(
            functools.partial(sweep_kernel, first, subs, order, columns),
            out_shape=[parcel] * 4 + [state],
            in_specs=[smem] * 4 + [vmem] * (3 + len(more)),
            out_specs=[vmem] * 5,
            scratch_shapes=[
                pltpu.VMEM((columns, length), jnp.float32),
                pltpu.VMEM((subs + 1, columns, order), jnp.bfloat16),
                rows,
                wide,
                pltpu.SMEM((subs,), jnp.int32),
                pltpu.SMEM((subs,), jnp.int32),
            ],
            compiler_params=params,
            name="sweep_first" if first else "sweep",
        )(chosen, destination, gap_count, index, dual, gap, right, *more)

    *sends, base = sweep(True)
    for step in range(ITERS):
        received = [lax.ppermute(part, axis, pairs) for part, (axis, pairs) in zip(sends, routes)]
        if step < ITERS - 1:
            *sends, base = sweep(False, base, *received)
    out = pl.pallas_call(
        functools.partial(last_kernel, subs, order, columns),
        out_shape=state,
        in_specs=[smem] + [vmem] * 5,
        out_specs=vmem,
        scratch_shapes=[rows, wide],
        compiler_params=params,
        name="last_update",
    )(index, base, *received)
    return out[None, None]


def solution(mesh):
    in_specs = (
        P("circ", "axial", None, None, None),
        P("circ", "axial", None, None, None),
        P("circ", "axial", None),
        P("circ", "axial", None),
        P("circ", "axial"),
        P("circ", "axial", None, None),
        P("circ", "axial", None, None),
    )
    out_specs = P("circ", "axial", None, None)
    return jax.shard_map(
        per_device, mesh=mesh, in_specs=in_specs, out_specs=out_specs, check_vma=False
    )
```

```python
import functools

import jax
import jax.numpy as jnp
from jax import lax
from jax.experimental import pallas as pl
from jax.experimental.pallas import tpu as pltpu
from jax.sharding import PartitionSpec as P

ITERS = 6
RELAXATION = 0.25
LANES = 128


def swap_pairs(count, first, closed):
    pairs = []
    for i in range(first, count, 2):
        if closed or i + 1 < count:
            j = (i + 1) % count
            pairs += [(i, j), (j, i)]
    return pairs


def scatter_face(index_ref, slot, received, wide, spread):
    face = wide.shape[0]
    packed = received[...].astype(jnp.float32)
    wide[0:face // 2] = packed
    wide[face // 2:] = pltpu.roll(packed, LANES // 2, 1)
    for j in range(face):
        spread[pl.ds(index_ref[slot * face + j], 1), :] = wide[j:j + 1, :]


def gather_face(index_ref, slot, send, wide, local):
    face = wide.shape[0]
    for j in range(face):
        wide[j:j + 1, :] = local[pl.ds(index_ref[slot * face + j], 1), :]
    low = wide[0:face // 2]
    high = pltpu.roll(wide[face // 2:], LANES // 2, 1)
    lane = lax.broadcasted_iota(jnp.int32, low.shape, 1)
    send[...] = jnp.where(lane < LANES // 2, low, high).astype(jnp.bfloat16)


def corrected(base_ref, spread, s, order, columns):
    block = spread[s * order:(s + 1) * order, :].T[:columns]
    return base_ref[:, s * order:(s + 1) * order] - RELAXATION * block


def products(subs, order, columns, list_ref, target_ref, count_ref, dual_ref, gap_ref, right_ref, iterate, rounded, slot_of, source_of, base_out, local):
    live = count_ref[0, 0]
    for g in range(subs):
        slot_of[target_ref[0, g]] = g
        source_of[target_ref[0, g]] = jnp.where(g < live, list_ref[0, g], subs)
    rounded[subs] = jnp.zeros_like(rounded[subs])
    for s in range(subs):
        product = jnp.dot(rounded[s], dual_ref[s], preferred_element_type=jnp.float32)
        product += jnp.dot(rounded[source_of[s]], gap_ref[slot_of[s]], preferred_element_type=jnp.float32)
        here = slice(s * order, (s + 1) * order)
        base_out[:, here] = iterate[:, here] + RELAXATION * (right_ref[:, here] - product)
        local[here, 0:columns] = product.T


def first_kernel(sizes, list_ref, target_ref, count_ref, index_ref, dual_ref, gap_ref, right_ref, send, base_out, local, spread, rounded, wide, slot_of, source_of):
    subs, order, columns = sizes
    for s in range(subs):
        rounded[s] = right_ref[:, s * order:(s + 1) * order].astype(jnp.bfloat16)
    products(*sizes, list_ref, target_ref, count_ref, dual_ref, gap_ref, right_ref, right_ref, rounded, slot_of, source_of, base_out, local)
    gather_face(index_ref, 0, send, wide, local)
    spread[...] = jnp.zeros_like(spread)


def sweep_kernel(sizes, list_ref, target_ref, count_ref, index_ref, dual_ref, gap_ref, right_ref, base_ref, part2, part3, spread_in, send, base_out, local, spread, iterate, rounded, wide, wide2, slot_of, source_of):
    subs, order, columns = sizes
    scatter_face(index_ref, 2, part2, wide, spread)
    scatter_face(index_ref, 3, part3, wide2, spread)
    for s in range(subs):
        value = corrected(base_ref, spread, s, order, columns)
        iterate[:, s * order:(s + 1) * order] = value
        rounded[s] = value.astype(jnp.bfloat16)
    products(*sizes, list_ref, target_ref, count_ref, dual_ref, gap_ref, right_ref, iterate, rounded, slot_of, source_of, base_out, local)
    gather_face(index_ref, 0, send, wide, local)


def early_kernel(index_ref, part0, part1, spread_in, spread, wide, wide2):
    scatter_face(index_ref, 0, part0, wide, spread)
    scatter_face(index_ref, 1, part1, wide2, spread)


def face_kernel(slot, index_ref, local, send, wide):
    gather_face(index_ref, slot, send, wide, local)


def last_kernel(sizes, index_ref, base_ref, part2, part3, spread_in, out_ref, spread, wide, wide2):
    subs, order, columns = sizes
    scatter_face(index_ref, 2, part2, wide, spread)
    scatter_face(index_ref, 3, part3, wide2, spread)
    for s in range(subs):
        out_ref[:, s * order:(s + 1) * order] = corrected(base_ref, spread, s, order, columns)


def per_device(dual_blocks, gap_blocks, gap_list, gap_target, gap_count, face_map, dual_right):
    columns, length = dual_right.shape[2:]
    subs, order = dual_blocks.shape[2:4]
    face = face_map.shape[3]
    dual, gap, right = dual_blocks[0, 0], gap_blocks[0, 0], dual_right[0, 0]
    chosen, destination = gap_list[0], gap_target[0]
    sizes = (subs, order, columns)
    n_circ, n_axial = lax.axis_size("circ"), lax.axis_size("axial")
    circ_odd = lax.axis_index("circ") % 2 == 1
    axial_odd = lax.axis_index("axial") % 2 == 1
    lower, upper, front, back = face_map[0, 0]
    index = jnp.concatenate([
        jnp.where(axial_odd, front, back),
        jnp.where(axial_odd, back, front),
        jnp.where(circ_odd, upper, lower),
        jnp.where(circ_odd, lower, upper),
    ])
    routes = [
        ("axial", swap_pairs(n_axial, 0, False)),
        ("axial", swap_pairs(n_axial, 1, False)),
        ("circ", swap_pairs(n_circ, 1, True)),
        ("circ", swap_pairs(n_circ, 0, True)),
    ]

    vmem = pl.BlockSpec(memory_space=pltpu.VMEM)
    smem = pl.BlockSpec(memory_space=pltpu.SMEM)
    parcel = jax.ShapeDtypeStruct((face // 2, LANES), jnp.bfloat16)
    state = jax.ShapeDtypeStruct((columns, length), jnp.float32)
    rows = jax.ShapeDtypeStruct((length, LANES), jnp.float32)
    wide = pltpu.VMEM((face, LANES), jnp.float32)
    rounded = pltpu.VMEM((subs + 1, columns, order), jnp.bfloat16)
    scalars = pltpu.SMEM((subs,), jnp.int32)
    params = pltpu.CompilerParams(vmem_limit_bytes=12 * 1024 * 1024)

    first = pl.pallas_call(
        functools.partial(first_kernel, sizes),
        out_shape=[parcel, state, rows, rows],
        in_specs=[smem] * 4 + [vmem] * 3,
        out_specs=[vmem] * 4,
        scratch_shapes=[rounded, wide, scalars, scalars],
        compiler_params=params,
        name="sweep_first",
    )
    sweep = pl.pallas_call(
        functools.partial(sweep_kernel, sizes),
        out_shape=[parcel, state, rows, rows],
        in_specs=[smem] * 4 + [vmem] * 7,
        out_specs=[vmem] * 4,
        scratch_shapes=[pltpu.VMEM(state.shape, jnp.float32), rounded, wide, wide, scalars, scalars],
        input_output_aliases={10: 3},
        compiler_params=params,
        name="sweep",
    )
    early = pl.pallas_call(
        early_kernel,
        out_shape=rows,
        in_specs=[smem] + [vmem] * 3,
        out_specs=vmem,
        scratch_shapes=[wide, wide],
        input_output_aliases={3: 0},
        compiler_params=params,
        name="scatter_early",
    )
    last = pl.pallas_call(
        functools.partial(last_kernel, sizes),
        out_shape=[state, rows],
        in_specs=[smem] + [vmem] * 4,
        out_specs=[vmem] * 2,
        scratch_shapes=[wide, wide],
        input_output_aliases={4: 1},
        compiler_params=params,
        name="last_update",
    )

    def face_values(slot, local):
        return pl.pallas_call(
            functools.partial(face_kernel, slot),
            out_shape=parcel,
            in_specs=[smem, vmem],
            out_specs=vmem,
            scratch_shapes=[wide],
            compiler_params=params,
            name=f"gather_{slot}",
        )(index, local)

    def swap(slot, send):
        return lax.ppermute(send, *routes[slot])

    send, base, local, spread = first(chosen, destination, gap_count, index, dual, gap, right)
    for step in range(ITERS):
        part0 = swap(0, send)
        part1 = swap(1, face_values(1, local))
        part2 = swap(2, face_values(2, local))
        part3 = swap(3, face_values(3, local))
        spread = early(index, part0, part1, spread)
        if step < ITERS - 1:
            send, base, local, spread = sweep(
                chosen, destination, gap_count, index, dual, gap, right, base, part2, part3, spread
            )
    out, _ = last(index, base, part2, part3, spread)
    return out[None, None]


def solution(mesh):
    in_specs = (
        P("circ", "axial", None, None, None),
        P("circ", "axial", None, None, None),
        P("circ", "axial", None),
        P("circ", "axial", None),
        P("circ", "axial"),
        P("circ", "axial", None, None),
        P("circ", "axial", None, None),
    )
    out_specs = P("circ", "axial", None, None)
    return jax.shard_map(
        per_device, mesh=mesh, in_specs=in_specs, out_specs=out_specs, check_vma=False
    )
```

```python
import functools

import jax
import jax.numpy as jnp
from jax import lax
from jax.experimental import pallas as pl
from jax.experimental.pallas import tpu as pltpu
from jax.sharding import PartitionSpec as P

ITERS = 6
RELAXATION = 0.25
LANES = 128
NOW = (0, 1)
LATER = ((2, 3),)
EARLY = ((0, 1),)
LAST = (2, 3)


def swap_pairs(count, first, closed):
    pairs = []
    for i in range(first, count, 2):
        if closed or i + 1 < count:
            j = (i + 1) % count
            pairs += [(i, j), (j, i)]
    return pairs


def scatter_face(index_ref, slot, received, wide, spread):
    face = wide.shape[0]
    packed = received[...].astype(jnp.float32)
    wide[0:face // 2] = packed
    wide[face // 2:] = pltpu.roll(packed, LANES // 2, 1)
    for j in range(face):
        spread[pl.ds(index_ref[slot * face + j], 1), :] = wide[j:j + 1, :]


def gather_face(index_ref, slot, send, wide, local):
    face = wide.shape[0]
    for j in range(face):
        wide[j:j + 1, :] = local[pl.ds(index_ref[slot * face + j], 1), :]
    low = wide[0:face // 2]
    high = pltpu.roll(wide[face // 2:], LANES // 2, 1)
    lane = lax.broadcasted_iota(jnp.int32, low.shape, 1)
    send[...] = jnp.where(lane < LANES // 2, low, high).astype(jnp.bfloat16)


def corrected(base_ref, spread, s, order, columns):
    block = spread[s * order:(s + 1) * order, :].T[:columns]
    return base_ref[:, s * order:(s + 1) * order] - RELAXATION * block


def targets_from(table_ref, start, subs, slot_of, source_of):
    live = table_ref[start + 2 * subs]
    for g in range(subs):
        target = table_ref[start + subs + g]
        if slot_of is not None:
            slot_of[target] = g
        source_of[target] = jnp.where(g < live, table_ref[start + g], subs)


def product_of(s, order, columns, dual_ref, gap_ref, right_ref, iterate, rounded, source_of, base_out, local):
    product = jnp.dot(rounded[s], dual_ref[s], preferred_element_type=jnp.float32)
    product += jnp.dot(rounded[source_of[s]], gap_ref[s], preferred_element_type=jnp.float32)
    here = slice(s * order, (s + 1) * order)
    base_out[:, here] = iterate[:, here] + RELAXATION * (right_ref[:, here] - product)
    local[here, 0:columns] = product.T


def first_kernel(sizes, slots, table_ref, dual_hbm, gap_hbm, right_hbm, *rest):
    subs, order, columns = sizes
    sends, rest = rest[:len(slots)], rest[len(slots):]
    base_out, local, spread, dual_ref, gap_ref, right_ref, rounded, wide, slot_of, source_of, sems = rest
    targets_from(table_ref, 4 * wide.shape[1], subs, slot_of, source_of)
    right_copy = pltpu.make_async_copy(right_hbm, right_ref, sems.at[2 * subs])
    right_copy.start()
    copies = []
    for s in range(subs):
        copies.append((
            pltpu.make_async_copy(dual_hbm.at[s], dual_ref.at[s], sems.at[2 * s]),
            pltpu.make_async_copy(gap_hbm.at[slot_of[s]], gap_ref.at[s], sems.at[2 * s + 1]),
        ))
        for copy in copies[-1]:
            copy.start()
    spread[...] = jnp.zeros_like(spread)
    right_copy.wait()
    for s in range(subs):
        rounded[s] = right_ref[:, s * order:(s + 1) * order].astype(jnp.bfloat16)
    rounded[subs] = jnp.zeros_like(rounded[subs])
    for s in range(subs):
        for copy in copies[s]:
            copy.wait()
        product_of(s, order, columns, dual_ref, gap_ref, right_ref, right_ref, rounded, source_of, base_out, local)
    for slot, send in zip(slots, sends):
        gather_face(table_ref, slot, send, wide.at[slot], local)


def sweep_kernel(sizes, slots, arrivals, table_ref, dual_ref, gap_ref, right_ref, base_ref, spread_in, *rest):
    subs, order, columns = sizes
    parts, rest = rest[:len(arrivals)], rest[len(arrivals):]
    sends, rest = rest[:len(slots)], rest[len(slots):]
    base_out, local, spread, iterate, rounded, wide, source_of = rest
    targets_from(table_ref, 4 * wide.shape[1], subs, None, source_of)
    for slot, part in zip(arrivals, parts):
        scatter_face(table_ref, slot, part, wide.at[slot], spread)
    for s in range(subs):
        value = corrected(base_ref, spread, s, order, columns)
        iterate[:, s * order:(s + 1) * order] = value
        rounded[s] = value.astype(jnp.bfloat16)
    rounded[subs] = jnp.zeros_like(rounded[subs])
    for s in range(subs):
        product_of(s, order, columns, dual_ref, gap_ref, right_ref, iterate, rounded, source_of, base_out, local)
    for slot, send in zip(slots, sends):
        gather_face(table_ref, slot, send, wide.at[slot], local)


def early_kernel(arrivals, table_ref, spread_in, *rest):
    parts, (spread, wide) = rest[:len(arrivals)], rest[len(arrivals):]
    for i, (slot, part) in enumerate(zip(arrivals, parts)):
        scatter_face(table_ref, slot, part, wide.at[i], spread)


def late_kernel(slots, table_ref, local, *rest):
    sends, wide = rest[:len(slots)], rest[len(slots)]
    for i, (slot, send) in enumerate(zip(slots, sends)):
        gather_face(table_ref, slot, send, wide.at[i], local)


def last_kernel(sizes, arrivals, table_ref, base_ref, spread_in, *rest):
    subs, order, columns = sizes
    parts, (out_ref, spread, wide) = rest[:len(arrivals)], rest[len(arrivals):]
    for i, (slot, part) in enumerate(zip(arrivals, parts)):
        scatter_face(table_ref, slot, part, wide.at[i], spread)
    for s in range(subs):
        out_ref[:, s * order:(s + 1) * order] = corrected(base_ref, spread, s, order, columns)


def per_device(dual_blocks, gap_blocks, gap_list, gap_target, gap_count, face_map, dual_right):
    columns, length = dual_right.shape[2:]
    subs, order = dual_blocks.shape[2:4]
    face = face_map.shape[3]
    dual, gap, right = dual_blocks[0, 0], gap_blocks[0, 0], dual_right[0, 0]
    sizes = (subs, order, columns)
    n_circ, n_axial = lax.axis_size("circ"), lax.axis_size("axial")
    circ_odd = lax.axis_index("circ") % 2 == 1
    axial_odd = lax.axis_index("axial") % 2 == 1
    lower, upper, front, back = face_map[0, 0]
    table = jnp.concatenate([
        jnp.where(axial_odd, front, back),
        jnp.where(axial_odd, back, front),
        jnp.where(circ_odd, upper, lower),
        jnp.where(circ_odd, lower, upper),
        gap_list[0, 0],
        gap_target[0, 0],
        gap_count[0],
    ])
    routes = [
        ("axial", swap_pairs(n_axial, 0, False)),
        ("axial", swap_pairs(n_axial, 1, False)),
        ("circ", swap_pairs(n_circ, 1, True)),
        ("circ", swap_pairs(n_circ, 0, True)),
    ]

    vmem = pl.BlockSpec(memory_space=pltpu.VMEM)
    smem = pl.BlockSpec(memory_space=pltpu.SMEM)
    hbm = pl.BlockSpec(memory_space=pltpu.HBM)
    parcel = jax.ShapeDtypeStruct((face // 2, LANES), jnp.bfloat16)
    state = jax.ShapeDtypeStruct((columns, length), jnp.float32)
    rows = jax.ShapeDtypeStruct((length, LANES), jnp.float32)
    blocks = jax.ShapeDtypeStruct(dual.shape, jnp.bfloat16)
    rounded = pltpu.VMEM((subs + 1, columns, order), jnp.bfloat16)
    scalars = pltpu.SMEM((subs,), jnp.int32)

    def wide(count):
        return pltpu.VMEM((count, face, LANES), jnp.float32)

    def call(kernel, name, specs, out_shape, scratch, aliases=None, grant=10):
        return jax.jit(pl.pallas_call(
            kernel,
            out_shape=out_shape,
            in_specs=specs,
            out_specs=[vmem] * len(out_shape),
            scratch_shapes=scratch,
            input_output_aliases=aliases or {},
            compiler_params=pltpu.CompilerParams(vmem_limit_bytes=grant * 1024 * 1024),
            name=name,
        ))

    first = call(
        functools.partial(first_kernel, sizes, NOW),
        "sweep_first",
        [smem] + [hbm] * 3,
        [parcel] * len(NOW) + [state, rows, rows, blocks, blocks, state],
        [rounded, wide(4), scalars, scalars, pltpu.SemaphoreType.DMA((2 * subs + 1,))],
        grant=21,
    )
    sweep = call(
        functools.partial(sweep_kernel, sizes, NOW, LAST),
        "sweep",
        [smem] + [vmem] * (5 + len(LAST)),
        [parcel] * len(NOW) + [state, rows, rows],
        [pltpu.VMEM(state.shape, jnp.float32), rounded, wide(4), scalars],
        {5: len(NOW) + 2},
    )
    late = {
        group: call(
            functools.partial(late_kernel, group),
            "gather_late",
            [smem, vmem],
            [parcel] * len(group),
            [wide(len(group))],
        )
        for group in LATER
    }
    early = {
        group: call(
            functools.partial(early_kernel, group),
            "scatter_early",
            [smem] + [vmem] * (1 + len(group)),
            [rows],
            [wide(len(group))],
            {1: 0},
        )
        for group in EARLY
    }
    last = call(
        functools.partial(last_kernel, sizes, LAST),
        "last_update",
        [smem] + [vmem] * (2 + len(LAST)),
        [state, rows],
        [wide(len(LAST))],
        {2: 1},
    )

    *sends, base, local, spread, dual, gap, right = first(table, dual, gap, right)
    for step in range(ITERS):
        parts = {slot: lax.ppermute(send, *routes[slot]) for slot, send in zip(NOW, sends)}
        for group in LATER:
            sends = late[group](table, local)
            parts |= {slot: lax.ppermute(send, *routes[slot]) for slot, send in zip(group, sends)}
        for group in EARLY:
            (spread,) = early[group](table, spread, *[parts[slot] for slot in group])
        arrived = [parts[slot] for slot in LAST]
        if step < ITERS - 1:
            *sends, base, local, spread = sweep(table, dual, gap, right, base, spread, *arrived)
    out, _ = last(table, base, spread, *arrived)
    return out[None, None]


def solution(mesh):
    in_specs = (
        P("circ", "axial", None, None, None),
        P("circ", "axial", None, None, None),
        P("circ", "axial", None),
        P("circ", "axial", None),
        P("circ", "axial"),
        P("circ", "axial", None, None),
        P("circ", "axial", None, None),
    )
    out_specs = P("circ", "axial", None, None)
    return jax.shard_map(
        per_device, mesh=mesh, in_specs=in_specs, out_specs=out_specs, check_vma=False
    )
```

```python
import functools

import jax
import jax.numpy as jnp
from jax import lax
from jax.experimental import pallas as pl
from jax.experimental.pallas import tpu as pltpu
from jax.sharding import PartitionSpec as P

ITERS = 6
RELAXATION = 0.25
LANES = 128
NOW = (0, 1)
LATER = ((2, 3),)
EARLY = ((0, 1),)
LAST = (2, 3)


def swap_pairs(count, first, closed):
    pairs = []
    for i in range(first, count, 2):
        if closed or i + 1 < count:
            j = (i + 1) % count
            pairs += [(i, j), (j, i)]
    return pairs


def scatter_face(index_ref, slot, received, wide, spread):
    face = wide.shape[0]
    packed = received[...].astype(jnp.float32)
    wide[0:face // 2] = packed
    wide[face // 2:] = pltpu.roll(packed, LANES // 2, 1)
    for j in range(face):
        spread[pl.ds(index_ref[slot * face + j], 1), :] = wide[j:j + 1, :]


def gather_face(index_ref, slot, send, wide, local):
    face = wide.shape[0]
    for j in range(face):
        wide[j:j + 1, :] = local[pl.ds(index_ref[slot * face + j], 1), :]
    low = wide[0:face // 2]
    high = pltpu.roll(wide[face // 2:], LANES // 2, 1)
    lane = lax.broadcasted_iota(jnp.int32, low.shape, 1)
    send[...] = jnp.where(lane < LANES // 2, low, high).astype(jnp.bfloat16)


def corrected(base_ref, spread, s, order, columns):
    block = spread[s * order:(s + 1) * order, :].T[:columns]
    return base_ref[:, s * order:(s + 1) * order] - RELAXATION * block


def targets_from(table_ref, start, subs, slot_of, source_of):
    live = table_ref[start + 2 * subs]
    for g in range(subs):
        target = table_ref[start + subs + g]
        if slot_of is not None:
            slot_of[target] = g
        source_of[target] = jnp.where(g < live, table_ref[start + g], subs)


def product_of(s, order, columns, dual_ref, gap_ref, right_ref, iterate, rounded, source_of, base_out, local):
    product = jnp.dot(rounded[s], dual_ref[s], preferred_element_type=jnp.float32)
    product += jnp.dot(rounded[source_of[s]], gap_ref[s], preferred_element_type=jnp.float32)
    here = slice(s * order, (s + 1) * order)
    base_out[:, here] = iterate[:, here] + RELAXATION * (right_ref[:, here] - product)
    local[here, 0:columns] = product.T


def first_kernel(sizes, slots, table_ref, dual_hbm, gap_hbm, right_hbm, *rest):
    subs, order, columns = sizes
    sends, rest = rest[:len(slots)], rest[len(slots):]
    base_out, local, spread, dual_ref, gap_ref, right_ref, rounded, wide, slot_of, source_of, sems = rest
    targets_from(table_ref, 4 * wide.shape[1], subs, slot_of, source_of)
    right_copy = pltpu.make_async_copy(right_hbm, right_ref, sems.at[2 * subs])
    right_copy.start()
    copies = []
    for s in range(subs):
        copies.append((
            pltpu.make_async_copy(dual_hbm.at[s], dual_ref.at[s], sems.at[2 * s]),
            pltpu.make_async_copy(gap_hbm.at[slot_of[s]], gap_ref.at[s], sems.at[2 * s + 1]),
        ))
        for copy in copies[-1]:
            copy.start()
    spread[...] = jnp.zeros_like(spread)
    right_copy.wait()
    for s in range(subs):
        rounded[s] = right_ref[:, s * order:(s + 1) * order].astype(jnp.bfloat16)
    rounded[subs] = jnp.zeros_like(rounded[subs])
    for s in range(subs):
        for copy in copies[s]:
            copy.wait()
        product_of(s, order, columns, dual_ref, gap_ref, right_ref, right_ref, rounded, source_of, base_out, local)
    for slot, send in zip(slots, sends):
        gather_face(table_ref, slot, send, wide.at[slot], local)


def sweep_kernel(sizes, slots, arrivals, table_ref, dual_ref, gap_ref, right_ref, base_ref, spread_in, *rest):
    subs, order, columns = sizes
    parts, rest = rest[:len(arrivals)], rest[len(arrivals):]
    sends, rest = rest[:len(slots)], rest[len(slots):]
    base_out, local, spread, iterate, rounded, wide, source_of = rest
    targets_from(table_ref, 4 * wide.shape[1], subs, None, source_of)
    for slot, part in zip(arrivals, parts):
        scatter_face(table_ref, slot, part, wide.at[slot], spread)
    for s in range(subs):
        value = corrected(base_ref, spread, s, order, columns)
        iterate[:, s * order:(s + 1) * order] = value
        rounded[s] = value.astype(jnp.bfloat16)
    rounded[subs] = jnp.zeros_like(rounded[subs])
    for s in range(subs):
        product_of(s, order, columns, dual_ref, gap_ref, right_ref, iterate, rounded, source_of, base_out, local)
    for slot, send in zip(slots, sends):
        gather_face(table_ref, slot, send, wide.at[slot], local)


def early_kernel(arrivals, table_ref, spread_in, *rest):
    parts, (spread, wide) = rest[:len(arrivals)], rest[len(arrivals):]
    for i, (slot, part) in enumerate(zip(arrivals, parts)):
        scatter_face(table_ref, slot, part, wide.at[i], spread)


def late_kernel(slots, table_ref, local, *rest):
    sends, wide = rest[:len(slots)], rest[len(slots)]
    for i, (slot, send) in enumerate(zip(slots, sends)):
        gather_face(table_ref, slot, send, wide.at[i], local)


def last_kernel(sizes, arrivals, table_ref, base_ref, spread_in, *rest):
    subs, order, columns = sizes
    parts, (out_hbm, spread, wide, result, sems) = rest[:len(arrivals)], rest[len(arrivals):]
    for i, (slot, part) in enumerate(zip(arrivals, parts)):
        scatter_face(table_ref, slot, part, wide.at[i], spread)
    copies = []
    for s in range(subs):
        here = slice(s * order, (s + 1) * order)
        result[:, here] = corrected(base_ref, spread, s, order, columns)
        copies.append(pltpu.make_async_copy(result.at[:, here], out_hbm.at[:, here], sems.at[s]))
        copies[-1].start()
    for copy in copies:
        copy.wait()


def per_device(dual_blocks, gap_blocks, gap_list, gap_target, gap_count, face_map, dual_right):
    columns, length = dual_right.shape[2:]
    subs, order = dual_blocks.shape[2:4]
    face = face_map.shape[3]
    dual, gap, right = dual_blocks[0, 0], gap_blocks[0, 0], dual_right[0, 0]
    sizes = (subs, order, columns)
    n_circ, n_axial = lax.axis_size("circ"), lax.axis_size("axial")
    circ_odd = lax.axis_index("circ") % 2 == 1
    axial_odd = lax.axis_index("axial") % 2 == 1
    lower, upper, front, back = face_map[0, 0]
    table = jnp.concatenate([
        jnp.where(axial_odd, front, back),
        jnp.where(axial_odd, back, front),
        jnp.where(circ_odd, upper, lower),
        jnp.where(circ_odd, lower, upper),
        gap_list[0, 0],
        gap_target[0, 0],
        gap_count[0],
    ])
    routes = [
        ("axial", swap_pairs(n_axial, 0, False)),
        ("axial", swap_pairs(n_axial, 1, False)),
        ("circ", swap_pairs(n_circ, 1, True)),
        ("circ", swap_pairs(n_circ, 0, True)),
    ]

    vmem = pl.BlockSpec(memory_space=pltpu.VMEM)
    smem = pl.BlockSpec(memory_space=pltpu.SMEM)
    hbm = pl.BlockSpec(memory_space=pltpu.HBM)
    parcel = jax.ShapeDtypeStruct((face // 2, LANES), jnp.bfloat16)
    state = jax.ShapeDtypeStruct((columns, length), jnp.float32)
    rows = jax.ShapeDtypeStruct((length, LANES), jnp.float32)
    blocks = jax.ShapeDtypeStruct(dual.shape, jnp.bfloat16)
    rounded = pltpu.VMEM((subs + 1, columns, order), jnp.bfloat16)
    scalars = pltpu.SMEM((subs,), jnp.int32)

    def wide(count):
        return pltpu.VMEM((count, face, LANES), jnp.float32)

    def call(kernel, name, specs, out_shape, scratch, aliases=None, grant=10, outs=None):
        return jax.jit(pl.pallas_call(
            kernel,
            out_shape=out_shape,
            in_specs=specs,
            out_specs=outs or [vmem] * len(out_shape),
            scratch_shapes=scratch,
            input_output_aliases=aliases or {},
            compiler_params=pltpu.CompilerParams(vmem_limit_bytes=grant * 1024 * 1024),
            name=name,
        ))

    first = call(
        functools.partial(first_kernel, sizes, NOW),
        "sweep_first",
        [smem] + [hbm] * 3,
        [parcel] * len(NOW) + [state, rows, rows, blocks, blocks, state],
        [rounded, wide(4), scalars, scalars, pltpu.SemaphoreType.DMA((2 * subs + 1,))],
        grant=21,
    )
    sweep = call(
        functools.partial(sweep_kernel, sizes, NOW, LAST),
        "sweep",
        [smem] + [vmem] * (5 + len(LAST)),
        [parcel] * len(NOW) + [state, rows, rows],
        [pltpu.VMEM(state.shape, jnp.float32), rounded, wide(4), scalars],
        {5: len(NOW) + 2},
    )
    late = {
        group: call(
            functools.partial(late_kernel, group),
            "gather_late",
            [smem, vmem],
            [parcel] * len(group),
            [wide(len(group))],
        )
        for group in LATER
    }
    early = {
        group: call(
            functools.partial(early_kernel, group),
            "scatter_early",
            [smem] + [vmem] * (1 + len(group)),
            [rows],
            [wide(len(group))],
            {1: 0},
        )
        for group in EARLY
    }
    last = call(
        functools.partial(last_kernel, sizes, LAST),
        "last_update",
        [smem] + [vmem] * (2 + len(LAST)),
        [state, rows],
        [wide(len(LAST)), pltpu.VMEM(state.shape, jnp.float32), pltpu.SemaphoreType.DMA((subs,))],
        {2: 1},
        outs=[hbm, vmem],
    )

    *sends, base, local, spread, dual, gap, right = first(table, dual, gap, right)
    for step in range(ITERS):
        parts = {slot: lax.ppermute(send, *routes[slot]) for slot, send in zip(NOW, sends)}
        for group in LATER:
            sends = late[group](table, local)
            parts |= {slot: lax.ppermute(send, *routes[slot]) for slot, send in zip(group, sends)}
        for group in EARLY:
            (spread,) = early[group](table, spread, *[parts[slot] for slot in group])
        arrived = [parts[slot] for slot in LAST]
        if step < ITERS - 1:
            *sends, base, local, spread = sweep(table, dual, gap, right, base, spread, *arrived)
    out, _ = last(table, base, spread, *arrived)
    return out[None, None]


def solution(mesh):
    in_specs = (
        P("circ", "axial", None, None, None),
        P("circ", "axial", None, None, None),
        P("circ", "axial", None),
        P("circ", "axial", None),
        P("circ", "axial"),
        P("circ", "axial", None, None),
        P("circ", "axial", None, None),
    )
    out_specs = P("circ", "axial", None, None)
    return jax.shard_map(
        per_device, mesh=mesh, in_specs=in_specs, out_specs=out_specs, check_vma=False
    )
```
